128 devices in a mesh: chain: 8 (over y, core), bond: 16 (over z, x).
Axes of the slice: x: 4, y: 4, z: 4, core: 2. Of those that a mesh axis runs over, the one named last changes fastest.
Arguments:
- wavefunction: bfloat16 [8, 16, 512, 512], P('chain', 'bond'), may hold values from -6 to 6
- left_env: bfloat16 [8, 16, 12, 512, 512], P('chain', 'bond'), may hold values from -0.25 to 0.25
- right_env: bfloat16 [8, 16, 12, 512, 512], P('chain', 'bond'), may hold values from -0.25 to 0.25
- source: int32 [8, 16, 12], P('chain', 'bond'), may hold values from 0 to 15
- block_sizes: int32 [8, 16], P('chain', 'bond'), may hold values from 128 to 512, as said below
- davidson_mix: float32 [8, 3, 3], P('chain'), may hold values from -0.5 to 0.5
- ritz_weights: float32 [8, 4], P('chain'), may hold values from 0.25 to 1
Outputs:
- updated: bfloat16 [8, 16, 512, 512], P('chain', 'bond')
- handed_env: bfloat16 [8, 16, 12, 512, 512], P('chain', 'bond')
The draws below stay inside these ranges and needn't reach their ends.
Inputs may be any that keep to these rules, and one draw needn't show every extreme that they name: `block_sizes`: in every section some sector's block is full.
All inputs are finite; a program needn't handle non-finite values.
Results may differ from the reference program's by a relative error of at most 0.025.
Values may be sent and summed in bfloat16 or wider, within the bound.
A program may use at most 128 MiB of HBM per device.

```python
import math
import jax
import jax.numpy as jnp
from jax import lax

BLK = 512
TERMS = 12
PRODUCTS = 3
SECTORS = 16
SECTIONS = 8


def draw_block_sizes(key, part):
    key = jax.random.fold_in(key, 7)
    key_sizes, key_full = jax.random.split(key)
    drawn = jax.random.randint(key_sizes, (SECTIONS, SECTORS), BLK // 4, BLK + 1)
    full_at = jax.random.randint(key_full, (SECTIONS, 1), 0, SECTORS)
    columns = jnp.arange(SECTORS)[None, :]
    return jnp.where(columns == full_at, BLK, drawn).astype(jnp.int32)


def set_ends(values, own_key, least, largest):
    extent = values.shape
    place = [jax.random.randint(jax.random.fold_in(own_key, axis), (), 0, extent[axis]) for axis in range(len(extent))]
    values = values.at[tuple(place)].set(least)
    longest = extent.index(max(extent))
    place[longest] = (place[longest] + 1) % extent[longest]
    return values.at[tuple(place)].set(largest)


def shard_levels(rng, shape, shards, low, high):
    gain = 1.0
    for position, shards_of in shards:
        draws = jax.random.uniform(jax.random.fold_in(jax.random.fold_in(rng, 6), position), (shards_of,), jnp.float32, low / len(shards), high / len(shards))
        gain = gain * jnp.repeat(jnp.exp(draws), shape[position] // shards_of).reshape((-1,) + (1,) * (len(shape) - 1 - position))
    return gain


def bell_draw(key, extent, spread, reach, cuts=(), held_as=jnp.bfloat16):
    values = spread * jax.random.normal(key, extent, jnp.float32)
    if cuts:
        values = values * shard_levels(key, extent, cuts, -0.22, 0.18)
    return jnp.clip(values, -reach, reach).astype(held_as)


def setup_inputs(seed: int = 0) -> dict:
    key_of = jax.random.split(jax.random.key(seed), 8)
    return {
        "wavefunction": bell_draw(key_of[0], (SECTIONS, SECTORS, BLK, BLK), 1.0, 6.0, ((0, 8), (1, 16))),
        "left_env": bell_draw(key_of[1], (SECTIONS, SECTORS, TERMS, BLK, BLK), BLK ** -0.5, 0.25, ((0, 8), (1, 16))),
        "right_env": bell_draw(key_of[2], (SECTIONS, SECTORS, TERMS, BLK, BLK), BLK ** -0.5, 0.25, ((0, 8), (1, 16))),
        "source": set_ends(jax.random.randint(key_of[3], (SECTIONS, SECTORS, TERMS), 0, SECTORS), jax.random.fold_in(key_of[3], 1), 0, SECTORS - 1).astype(jnp.int32),
        "block_sizes": draw_block_sizes(jax.random.fold_in(key_of[7], 71), 0),
        "davidson_mix": jnp.clip(jax.random.uniform(key_of[5], (SECTIONS, PRODUCTS, PRODUCTS), jnp.float32, -0.5, 0.5) * shard_levels(key_of[5], (SECTIONS, PRODUCTS, PRODUCTS), ((0, 8),), -0.4, 0.0), -0.5, 0.5),
        "ritz_weights": jnp.clip(0.25 + 0.75 * jax.random.uniform(key_of[6], (SECTIONS, PRODUCTS + 1), jnp.float32) ** shard_levels(key_of[6], (SECTIONS, PRODUCTS + 1), ((0, 8),), -0.2, 0.2), 0.25, 1.0),
    }


EPSILON = 1e-06

def live_mask(block_sizes):
    counter = jnp.arange(BLK, dtype=jnp.int32)
    row_live = (counter[None, :] < block_sizes[:, None]).astype(jnp.float32)
    return row_live[:, :, None] * row_live[:, None, :]

def one_section(operands):
    wavefunction, left_env, right_env, source, block_sizes, davidson_mix, ritz_weights = operands
    masking = live_mask(block_sizes)
    entries = float(SECTORS * BLK * BLK)

    def rescale(value):
        return (value * lax.rsqrt(jnp.sum(value * value) / entries + EPSILON)).astype(jnp.bfloat16)

    def apply_hamiltonian(vector):
        picked = vector[source]
        halfway = jnp.einsum('stij,stjk->stik', left_env.astype(jnp.float32), picked.astype(jnp.float32)).astype(jnp.bfloat16)
        applied = jnp.einsum('stik,stlk->sil', halfway.astype(jnp.float32), right_env.astype(jnp.float32))
        return applied * masking
    vectors = [rescale(wavefunction.astype(jnp.float32) * masking)]
    for number in range(PRODUCTS):
        residual = apply_hamiltonian(vectors[number])
        for other in range(number + 1):
            residual = residual - davidson_mix[number, other] * vectors[other].astype(jnp.float32)
        vectors.append(rescale(residual))
    combined = jnp.zeros((SECTORS, BLK, BLK), jnp.float32)
    for number in range(PRODUCTS + 1):
        combined = combined + ritz_weights[number] * vectors[number].astype(jnp.float32)
    updated = rescale(combined)
    picked = updated[source]
    grown_half = jnp.einsum('smi,stmj->stij', updated.astype(jnp.float32), left_env.astype(jnp.float32)).astype(jnp.bfloat16)
    grown = jnp.einsum('stij,stjk->stik', grown_half.astype(jnp.float32), picked.astype(jnp.float32))
    grown = (grown * (1.0 / math.sqrt(BLK))).astype(jnp.bfloat16)
    return (updated, grown)

def reference(wavefunction, left_env, right_env, source, block_sizes, davidson_mix, ritz_weights):
    updated, grown = lax.map(one_section, (wavefunction, left_env, right_env, source, block_sizes, davidson_mix, ritz_weights))
    handed_env = jnp.concatenate([jnp.zeros_like(grown[:1]), grown[:-1]], axis=0)
    return (updated, handed_env)
```

```python
import math

import jax
import jax.numpy as jnp
from jax import lax
from jax.experimental import pallas as pl
from jax.experimental.pallas import tpu as pltpu
from jax.sharding import PartitionSpec as P

PRODUCTS = 3
EPSILON = 1e-06
MESH = pl.DeviceIdType.MESH
RING = 4
LANES = 128
F32 = jnp.float32
BF16 = jnp.bfloat16

ORDER = (
    (("E", 1, 0), ("E", 1, 1), ("E", 2, 0), ("E", 1, 2), ("E", 3, 0), ("E", 2, 1), ("E", 1, 3), ("E", 4, 0))
    + (("C", 0, 0), ("E", 3, 1), ("C", 0, 1), ("E", 2, 2), ("C", 0, 2), ("E", 4, 1), ("C", 0, 3), ("S", 0))
    + (("E", 3, 2), ("C", 1, 0), ("C", 1, 1), ("E", 2, 3), ("C", 1, 2), ("C", 1, 3), ("S", 1), ("E", 4, 2))
    + (("C", 2, 0), ("E", 3, 3), ("C", 2, 1), ("C", 2, 2), ("C", 2, 3), ("S", 2), ("E", 4, 3))
)
EARLY = (("E", 1, 0), ("E", 1, 1), ("E", 2, 0), ("E", 1, 2))

TURN = ("E", 4, 0)


class Gather:
    def __init__(self, parts, send, recv, z, x, width):
        self.parts, self.send, self.recv = parts, send, recv
        self.z, self.x = z, x
        self.me = z * RING + x
        self.half = width // 2
        self.quarter = width // 4

    def sector(self, path, first, second):
        a, b = (self.x, self.z) if path == 0 else (self.z, self.x)
        a = lax.rem(a + (first + RING), RING)
        b = lax.rem(b + (second + RING), RING)
        return b * RING + a if path == 0 else a * RING + b

    def copy(self, part, path, sector, offset, rows, device, slot):
        ref = self.parts[part].at[sector, pl.ds(path * self.half + offset, rows), :]
        return pltpu.make_async_remote_copy(
            src_ref=ref,
            dst_ref=ref,
            send_sem=self.send.at[part],
            recv_sem=self.recv.at[part, path, slot],
            device_id={"bond": device},
            device_id_type=MESH,
        )

    OFFSETS = (0, 1, -1, 2)

    def own_first(self, part, path):
        for slot, way in ((0, 1), (1, -1)):
            self.copy(part, path, self.me, 0, self.half, self.sector(path, way, 0), slot).start()

    def own_second(self, part, path, which):
        sector = self.sector(path, self.OFFSETS[which], 0)
        for side, way in ((0, 1), (1, -1)):
            slot = 4 + 4 * which + side
            self.copy(part, path, sector, 0, self.half, self.sector(path, 0, way), slot).start()

    def pass_first(self, part, path, side):
        way = 1 if side == 0 else -1
        sector = self.sector(path, -way, 0)
        self.copy(part, path, sector, 0, self.half, self.me, side).wait_recv()
        target = self.sector(path, way, 0)
        self.copy(part, path, sector, self.quarter * side, self.quarter, target, 2 + side).start()

    def end_first(self, part, path):
        sector = self.sector(path, 2, 0)
        for side in (0, 1):
            self.copy(part, path, sector, self.quarter * side, self.quarter, self.me, 2 + side).wait_recv()

    def pass_second(self, part, path, which, side):
        way = 1 if side == 0 else -1
        sector = self.sector(path, self.OFFSETS[which], -way)
        slot = 4 + 4 * which + side
        self.copy(part, path, sector, 0, self.half, self.me, slot).wait_recv()
        target = self.sector(path, 0, way)
        self.copy(part, path, sector, self.quarter * side, self.quarter, target, slot + 2).start()

    def end_second(self, part, path, which):
        sector = self.sector(path, self.OFFSETS[which], 2)
        for side in (0, 1):
            slot = 4 + 4 * which + 2 + side
            self.copy(part, path, sector, self.quarter * side, self.quarter, self.me, slot).wait_recv()

    def stage(self, number, part):
        if number == 0:
            for path in (0, 1):
                self.own_first(part, path)
            for path in (0, 1):
                self.own_second(part, path, 0)
        elif number == 1:
            for side in (0, 1):
                for path in (0, 1):
                    self.pass_first(part, path, side)
                    self.own_second(part, path, 2 if side == 0 else 1)
            for side in (0, 1):
                for path in (0, 1):
                    self.pass_second(part, path, 0, side)
        elif number == 2:
            for path in (0, 1):
                self.end_first(part, path)
                self.own_second(part, path, 3)
            for which in (1, 2):
                for side in (0, 1):
                    for path in (0, 1):
                        self.pass_second(part, path, which, side)
        elif number == 3:
            for side in (0, 1):
                for path in (0, 1):
                    self.pass_second(part, path, 3, side)
        else:
            for path in (0, 1):
                for which in range(4):
                    self.end_second(part, path, which)

    def sent(self, part):
        ref = self.parts[part].at[pl.ds(0, RING * RING - 1)]
        pltpu.make_async_remote_copy(
            src_ref=ref,
            dst_ref=ref,
            send_sem=self.send.at[part],
            recv_sem=self.recv.at[part, 0, 0],
            device_id={"bond": self.me},
            device_id_type=MESH,
        ).wait_send()


def kernel(
    wave_ref,
    left_ref,
    right_ref,
    source_ref,
    sizes_ref,
    mixing_hbm,
    weights_ref,
    updated_ref,
    handed_ref,
    *scratch,
):
    terms, width = left_ref.shape[2], left_ref.shape[3]
    count = width // LANES
    group = terms // 4
    parts = (scratch[:count], scratch[count : 2 * count])
    (
        left,
        right,
        turned,
        landed_left,
        half,
        total,
        own,
        combined,
        handed_vector,
        flipped,
        norm_own,
        norm_first,
        norm_row,
        norm_second,
        norm_all,
        norm_landed,
        source_tile,
        source_landed,
        source_before,
        mixing_ref,
        load_sem,
        send_sem,
        recv_sem,
        norm_send,
        norm_recv,
        chain_send,
        chain_recv,
        local_sem,
        out_sem,
        turn_sem,
    ) = scratch[2 * count :]
    chain = lax.axis_index("chain")
    bond = lax.axis_index("bond")
    chains = lax.axis_size("chain")
    z, x = lax.div(bond, RING), lax.rem(bond, RING)
    after = lax.rem(chain + 1, chains)
    before = lax.rem(chain + chains - 1, chains)
    entries = float(RING * RING * width * width)

    load_left = pltpu.make_async_copy(left_ref.at[0, 0], left, load_sem.at[0])
    load_right = pltpu.make_async_copy(right_ref.at[0, 0], right, load_sem.at[1])
    load_left.start()
    load_right.start()
    load_mixing = pltpu.make_async_copy(mixing_hbm, mixing_ref, load_sem.at[2])
    load_mixing.start()

    def along_x(by):
        return z * RING + lax.rem(x + by, RING)

    def along_z(by):
        return lax.rem(z + by, RING) * RING + x

    barrier = pltpu.get_barrier_semaphore()
    for by in range(1, RING):
        for device in (along_x(by), along_z(by)):
            pl.semaphore_signal(barrier, inc=1, device_id={"bond": device}, device_id_type=MESH)
    for device in (after, before):
        pl.semaphore_signal(barrier, inc=1, device_id={"chain": device}, device_id_type=MESH)

    size = sizes_ref[0, 0]
    row_live = lax.broadcasted_iota(jnp.int32, (width, LANES), 0) < size

    def masked(value, part):
        column = lax.broadcasted_iota(jnp.int32, (width, LANES), 1) + part * LANES
        return jnp.where(row_live & (column < size), value, 0.0)

    def columns(part):
        return pl.ds(part * LANES, LANES)

    def tile_sum(value):
        return jnp.sum((value * value).reshape(width // 8, 8, LANES), axis=0)

    gathers = [
        Gather(parts[number % 2], send_sem.at[number % 2], recv_sem.at[number % 2], z, x, width)
        for number in range(PRODUCTS + 1)
    ]

    def to_chain(src, dst, slot):
        return pltpu.make_async_remote_copy(
            src_ref=src,
            dst_ref=dst,
            send_sem=chain_send.at[slot],
            recv_sem=chain_recv.at[slot],
            device_id={"chain": after},
            device_id_type=MESH,
        )

    def norm_copy(number, phase, by):
        return pltpu.make_async_remote_copy(
            src_ref=(norm_own if phase == 0 else norm_row).at[number],
            dst_ref=(norm_first if phase == 0 else norm_second).at[number, by - 1],
            send_sem=norm_send.at[number, phase, by - 1],
            recv_sem=norm_recv.at[number, phase, by - 1],
            device_id={"bond": along_x(by) if phase == 0 else along_z(by)},
            device_id_type=MESH,
        )

    def norm_start(number, tile):
        norm_own[number] = tile
        for by in range(1, RING):
            norm_copy(number, 0, by).start()

    def norm_middle(number):
        for by in range(1, RING):
            norm_copy(number, 0, by).wait_recv()
        norm_row[number] = norm_own[number] + norm_first[number, 0] + norm_first[number, 1] + norm_first[number, 2]
        for by in range(1, RING):
            norm_copy(number, 1, by).start()

    def scale_of(tile):
        summed = jnp.sum(jnp.sum(tile, axis=0, keepdims=True), axis=1, keepdims=True)
        return lax.rsqrt(summed / entries + EPSILON)

    def norm_end(number):
        for by in range(1, RING):
            norm_copy(number, 1, by).wait_recv()
        norm_all[number] = (
            norm_row[number] + norm_second[number, 0] + norm_second[number, 1] + norm_second[number, 2]
        )
        return scale_of(norm_all[number])

    def place(number, part, value):
        own[number, part] = value
        parts[number % 2][part][bond] = value

    values = []
    squares = jnp.zeros((8, LANES), F32)
    for part in range(count):
        value = masked(wave_ref[0, 0, :, columns(part)].astype(F32), part)
        squares = squares + tile_sum(value)
        place(0, part, value.astype(BF16))
    lane = lax.broadcasted_iota(jnp.int32, (8, LANES), 1)
    tile = jnp.zeros((8, LANES), jnp.int32)
    for term in range(terms):
        tile = jnp.where(lane == term, source_ref[0, 0, term], tile)
    source_tile[...] = tile

    pl.semaphore_wait(barrier, 2 * (RING - 1) + 2)
    odd = lax.rem(chain, 2) == 1

    @pl.when(odd)
    def _():
        pl.semaphore_wait(turn_sem, 1)

    gathers[0].stage(0, 0)
    norm_start(0, squares)
    for part in range(1, count):
        gathers[0].stage(0, part)
    send_source = to_chain(source_tile, source_landed, 0)
    send_source.start()
    send_left = to_chain(left_ref.at[0, 0], landed_left, 1)
    send_left.start()

    def turn(number):
        def step(term, carry):
            for part in range(count):
                rows = pl.ds(pl.multiple_of(term * LANES, LANES), LANES)
                turned[part, rows, :] = jnp.transpose(right[term, :, columns(part)])
            return carry

        lax.fori_loop(number * group, (number + 1) * group, step, 0)

    def halves(number, part, which):
        held = parts[number % 2][part]

        for term in range(which * group, (which + 1) * group):
            block = held[source_ref[0, 0, term]]
            product = jnp.dot(left[term], block, preferred_element_type=F32)
            half[:, columns(term)] = product.astype(BF16)

    def gather_sum(part, side):
        wide = pl.ds(side * (width // 2), width // 2)
        product = jnp.dot(half[...], turned[part, :, wide], preferred_element_type=F32)
        if part == 0:
            total[:, wide] = product
        else:
            total[:, wide] += product

    scales = []
    for number in range(PRODUCTS):
        here = gathers[number]
        for item in ORDER:
            if item[0] == "E":
                here.stage(*item[1:])
                if item == EARLY[0]:
                    norm_middle(number)
                if number == 0 and item == TURN:

                    @pl.when(jnp.logical_not(odd))
                    def _():
                        pl.semaphore_signal(turn_sem, inc=1, device_id={"chain": after}, device_id_type=MESH)

                if number == 0 and item in EARLY:
                    if item == EARLY[0]:
                        load_right.wait()
                    turn(EARLY.index(item))
                if number == 0 and item == ("E", 4, 0):
                    load_left.wait()
                    load_mixing.wait()
            elif item[0] == "C":
                halves(number, *item[1:])
            else:
                for side in (0, 1):
                    gather_sum(item[1], side)
        scales.append(norm_end(number))
        for which in range(4):
            halves(number, count - 1, which)
        for part in range(count):
            here.sent(part)
        squares = jnp.zeros((8, LANES), F32)
        for side in (0, 1):
            gather_sum(count - 1, side)
            for part in range(side * count // 2, (side + 1) * count // 2):
                value = scales[number] * masked(total[:, columns(part)], part)
                for other in range(number + 1):
                    factor = mixing_ref[0, number : number + 1, other : other + 1] * scales[other]
                    value = value - factor * own[other, part].astype(F32)
                squares = squares + tile_sum(value)
                if number + 1 < PRODUCTS:
                    place(number + 1, part, value.astype(BF16))
                    gathers[number + 1].stage(0, part)
                else:
                    combined[:, columns(part)] = value
        norm_start(number + 1, squares)

    norm_middle(PRODUCTS)
    last = norm_end(PRODUCTS)
    squares = jnp.zeros((8, LANES), F32)
    for part in range(count):
        value = (weights_ref[0, PRODUCTS] * last) * combined[:, columns(part)]
        for other in range(PRODUCTS):
            value = value + (weights_ref[0, other] * scales[other]) * own[other, part].astype(F32)
        combined[:, columns(part)] = value
        own[PRODUCTS, part] = value.astype(BF16)
        to_chain(own.at[PRODUCTS, part], handed_vector.at[part], 3 + part).start()
        squares = squares + tile_sum(value)
    norm_start(PRODUCTS + 1, squares)

    here = gathers[PRODUCTS]
    for part in range(count):
        to_chain(own.at[PRODUCTS, part], handed_vector.at[part], 3 + part).wait_recv()
        parts[PRODUCTS % 2][part][bond] = handed_vector[part]
        here.stage(0, part)
    norm_middle(PRODUCTS + 1)
    send_source.wait_recv()
    fetch_source = pltpu.make_async_copy(source_landed, source_before, local_sem)
    fetch_source.start()
    for part in range(count):
        flipped[pl.ds(part * LANES, LANES), :] = jnp.transpose(handed_vector[part])
    fetch_source.wait()
    send_left.wait_recv()

    def grow_half(which):
        for term in range(which * group, (which + 1) * group):
            product = jnp.dot(flipped[...], landed_left[term], preferred_element_type=F32)
            right[term] = product.astype(BF16)

    def out_copy(part):
        return pltpu.make_async_copy(
            left.at[:, :, columns(part)], handed_ref.at[0, 0, :, :, columns(part)], out_sem.at[part]
        )

    def grow(part, which, factor):
        held = parts[PRODUCTS % 2][part]

        for term in range(which * group, (which + 1) * group):
            block = held[source_before[0, term]]
            product = jnp.dot(right[term], block, preferred_element_type=F32)
            left[term, :, columns(part)] = (product * factor).astype(BF16)

    factor = None
    for item in ORDER:
        if item[0] == "E":
            here.stage(*item[1:])
            if item in EARLY:
                grow_half(EARLY.index(item))
            if item == EARLY[0]:
                scale = norm_end(PRODUCTS + 1)
                send_norm = to_chain(norm_all.at[PRODUCTS + 1], norm_landed, 2)
                send_norm.start()
                for column in range(count):
                    updated_ref[0, 0, :, columns(column)] = (scale * combined[:, columns(column)]).astype(BF16)
            if item == ("E", 3, 0):
                send_norm.wait_recv()
                scale = scale_of(norm_landed[...])
                factor = scale * scale * (1.0 / math.sqrt(width))
                factor = jnp.where(chain > 0, factor, jnp.zeros_like(factor))
        elif item[0] == "C":
            grow(*item[1:], factor)
        else:
            out_copy(item[1]).start()
    for which in range(4):
        grow(count - 1, which, factor)
    out_copy(count - 1).start()
    for part in range(count):
        here.sent(part)
    for number in range(PRODUCTS + 2):
        for phase in (0, 1):
            for by in range(1, RING):
                norm_copy(number, phase, by).wait_send()
    send_source.wait_send()
    send_left.wait_send()
    send_norm.wait_send()
    for part in range(count):
        to_chain(own.at[PRODUCTS, part], handed_vector.at[part], 3 + part).wait_send()
    for part in range(count):
        out_copy(part).wait()


def keep_kernel(updated_ref, handed_ref, updated_out, handed_out, rest, rest_updated, load, store):
    loads = [pltpu.make_async_copy(updated_ref, rest_updated, load.at[0])]
    stores = [pltpu.make_async_copy(rest_updated, updated_out, store.at[0])]
    for term in range(handed_ref.shape[2]):
        loads.append(pltpu.make_async_copy(handed_ref.at[0, 0, term], rest.at[term], load.at[term + 1]))
        stores.append(pltpu.make_async_copy(rest.at[term], handed_out.at[0, 0, term], store.at[term + 1]))
    for copy in loads:
        copy.start()
    for first, second in zip(loads, stores):
        first.wait()
        second.start()
    for copy in stores:
        copy.wait()


def keep(updated, handed):
    anywhere = pl.BlockSpec(memory_space=pl.ANY)
    copies = handed.shape[2] + 1
    return pl.pallas_call(
        keep_kernel,
        out_shape=(
            jax.ShapeDtypeStruct(updated.shape, BF16),
            jax.ShapeDtypeStruct(handed.shape, BF16),
        ),
        in_specs=[anywhere, anywhere],
        out_specs=(anywhere, anywhere),
        scratch_shapes=[
            pltpu.VMEM(handed.shape[2:], BF16),
            pltpu.VMEM(updated.shape, BF16),
            pltpu.SemaphoreType.DMA((copies,)),
            pltpu.SemaphoreType.DMA((copies,)),
        ],
        compiler_params=pltpu.CompilerParams(vmem_limit_bytes=60 * 2**20),
        name="keep",
    )(updated, handed)


def body(wavefunction, left_env, right_env, source, block_sizes, davidson_mix, ritz_weights):
    terms, width = left_env.shape[2], left_env.shape[3]
    count = width // LANES
    blocks = (terms, width, width)
    vmem, smem, anywhere = (pl.BlockSpec(memory_space=space) for space in (pltpu.VMEM, pltpu.SMEM, pl.ANY))
    tile = (8, LANES)
    norms = PRODUCTS + 2
    scratch = [pltpu.VMEM((RING * RING, width, LANES), BF16) for _ in range(2 * count)] + [
        pltpu.VMEM(blocks, BF16),
        pltpu.VMEM(blocks, BF16),
        pltpu.VMEM((count, terms * LANES, width), BF16),
        pltpu.VMEM(blocks, BF16),
        pltpu.VMEM((width, terms * LANES), BF16),
        pltpu.VMEM((width, width), F32),
        pltpu.VMEM((PRODUCTS + 1, count, width, LANES), BF16),
        pltpu.VMEM((width, width), F32),
        pltpu.VMEM((count, width, LANES), BF16),
        pltpu.VMEM((width, width), BF16),
        pltpu.VMEM((norms,) + tile, F32),
        pltpu.VMEM((norms, RING - 1) + tile, F32),
        pltpu.VMEM((norms,) + tile, F32),
        pltpu.VMEM((norms, RING - 1) + tile, F32),
        pltpu.VMEM((norms,) + tile, F32),
        pltpu.VMEM(tile, F32),
        pltpu.VMEM(tile, jnp.int32),
        pltpu.VMEM(tile, jnp.int32),
        pltpu.SMEM(tile, jnp.int32),
        pltpu.VMEM(davidson_mix.shape, F32),
        pltpu.SemaphoreType.DMA((3,)),
        pltpu.SemaphoreType.DMA((2, count)),
        pltpu.SemaphoreType.DMA((2, count, 2, 20)),
        pltpu.SemaphoreType.DMA((norms, 2, RING - 1)),
        pltpu.SemaphoreType.DMA((norms, 2, RING - 1)),
        pltpu.SemaphoreType.DMA((3 + count,)),
        pltpu.SemaphoreType.DMA((3 + count,)),
        pltpu.SemaphoreType.DMA,
        pltpu.SemaphoreType.DMA((count,)),
        pltpu.SemaphoreType.REGULAR,
    ]
    flops = (PRODUCTS + 1) * 2 * terms * 2 * width**3
    updated, handed = pl.pallas_call(
        kernel,
        out_shape=(
            jax.ShapeDtypeStruct(wavefunction.shape, BF16),
            jax.ShapeDtypeStruct(left_env.shape, BF16),
        ),
        in_specs=[vmem, anywhere, anywhere, smem, smem, anywhere, smem],
        out_specs=(vmem, anywhere),
        scratch_shapes=scratch,
        compiler_params=pltpu.CompilerParams(
            collective_id=0, has_side_effects=True, vmem_limit_bytes=60 * 2**20
        ),
        cost_estimate=pl.CostEstimate(flops=flops, bytes_accessed=40 * 2**20, transcendentals=0),
        name="davidson_update",
    )(wavefunction, left_env, right_env, source, block_sizes, davidson_mix, ritz_weights)
    return keep(updated, handed)


def solution(mesh):
    in_specs = (
        P("chain", "bond", None, None),
        P("chain", "bond", None, None, None),
        P("chain", "bond", None, None, None),
        P("chain", "bond", None),
        P("chain", "bond"),
        P("chain", None, None),
        P("chain", None),
    )
    out_specs = (P("chain", "bond", None, None), P("chain", "bond", None, None, None))
    return jax.shard_map(body, mesh=mesh, in_specs=in_specs, out_specs=out_specs, check_vma=False)
```

```python
import math

import jax
import jax.numpy as jnp
from jax import lax
from jax.experimental import pallas as pl
from jax.experimental.pallas import tpu as pltpu
from jax.sharding import PartitionSpec as P

PRODUCTS = 3
EPSILON = 1e-06
MESH = pl.DeviceIdType.MESH
RING = 4
LANES = 128
F32 = jnp.float32
BF16 = jnp.bfloat16

ORDER = (
    (("E", 1, 0), ("E", 1, 1), ("E", 2, 0), ("E", 1, 2), ("E", 3, 0), ("E", 2, 1), ("E", 1, 3), ("E", 4, 0))
    + (("C", 0, 0), ("E", 3, 1), ("C", 0, 1), ("E", 2, 2), ("C", 0, 2), ("E", 4, 1), ("C", 0, 3), ("S", 0))
    + (("E", 3, 2), ("C", 1, 0), ("C", 1, 1), ("E", 2, 3), ("C", 1, 2), ("C", 1, 3), ("S", 1), ("E", 4, 2))
    + (("C", 2, 0), ("E", 3, 3), ("C", 2, 1), ("C", 2, 2), ("C", 2, 3), ("S", 2), ("E", 4, 3))
)
EARLY = (("E", 1, 0), ("E", 1, 1), ("E", 2, 0), ("E", 1, 2))

TURN = ("E", 4, 0)


class Gather:
    def __init__(self, parts, send, recv, z, x, width):
        self.parts, self.send, self.recv = parts, send, recv
        self.z, self.x = z, x
        self.me = z * RING + x
        self.half = width // 2
        self.quarter = width // 4

    def sector(self, path, first, second):
        a, b = (self.x, self.z) if path == 0 else (self.z, self.x)
        a = lax.rem(a + (first + RING), RING)
        b = lax.rem(b + (second + RING), RING)
        return b * RING + a if path == 0 else a * RING + b

    def copy(self, part, path, sector, offset, rows, device, slot):
        ref = self.parts[part].at[sector, pl.ds(path * self.half + offset, rows), :]
        return pltpu.make_async_remote_copy(
            src_ref=ref,
            dst_ref=ref,
            send_sem=self.send.at[part],
            recv_sem=self.recv.at[part, path, slot],
            device_id={"bond": device},
            device_id_type=MESH,
        )

    OFFSETS = (0, 1, -1, 2)

    def own_first(self, part, path):
        for slot, way in ((0, 1), (1, -1)):
            self.copy(part, path, self.me, 0, self.half, self.sector(path, way, 0), slot).start()

    def own_second(self, part, path, which):
        sector = self.sector(path, self.OFFSETS[which], 0)
        for side, way in ((0, 1), (1, -1)):
            slot = 4 + 4 * which + side
            self.copy(part, path, sector, 0, self.half, self.sector(path, 0, way), slot).start()

    def pass_first(self, part, path, side):
        way = 1 if side == 0 else -1
        sector = self.sector(path, -way, 0)
        self.copy(part, path, sector, 0, self.half, self.me, side).wait_recv()
        target = self.sector(path, way, 0)
        self.copy(part, path, sector, self.quarter * side, self.quarter, target, 2 + side).start()

    def end_first(self, part, path):
        sector = self.sector(path, 2, 0)
        for side in (0, 1):
            self.copy(part, path, sector, self.quarter * side, self.quarter, self.me, 2 + side).wait_recv()

    def pass_second(self, part, path, which, side):
        way = 1 if side == 0 else -1
        sector = self.sector(path, self.OFFSETS[which], -way)
        slot = 4 + 4 * which + side
        self.copy(part, path, sector, 0, self.half, self.me, slot).wait_recv()
        target = self.sector(path, 0, way)
        self.copy(part, path, sector, self.quarter * side, self.quarter, target, slot + 2).start()

    def end_second(self, part, path, which):
        sector = self.sector(path, self.OFFSETS[which], 2)
        for side in (0, 1):
            slot = 4 + 4 * which + 2 + side
            self.copy(part, path, sector, self.quarter * side, self.quarter, self.me, slot).wait_recv()

    def stage(self, number, part):
        if number == 0:
            for path in (0, 1):
                self.own_first(part, path)
            for path in (0, 1):
                self.own_second(part, path, 0)
        elif number == 1:
            for side in (0, 1):
                for path in (0, 1):
                    self.pass_first(part, path, side)
                    self.own_second(part, path, 2 if side == 0 else 1)
            for side in (0, 1):
                for path in (0, 1):
                    self.pass_second(part, path, 0, side)
        elif number == 2:
            for path in (0, 1):
                self.end_first(part, path)
                self.own_second(part, path, 3)
            for which in (1, 2):
                for side in (0, 1):
                    for path in (0, 1):
                        self.pass_second(part, path, which, side)
        elif number == 3:
            for side in (0, 1):
                for path in (0, 1):
                    self.pass_second(part, path, 3, side)
        else:
            for path in (0, 1):
                for which in range(4):
                    self.end_second(part, path, which)

    def sent(self, part):
        ref = self.parts[part].at[pl.ds(0, RING * RING - 1)]
        pltpu.make_async_remote_copy(
            src_ref=ref,
            dst_ref=ref,
            send_sem=self.send.at[part],
            recv_sem=self.recv.at[part, 0, 0],
            device_id={"bond": self.me},
            device_id_type=MESH,
        ).wait_send()


def kernel(
    wave_ref,
    left_ref,
    right_ref,
    source_ref,
    sizes_ref,
    mixing_hbm,
    weights_ref,
    updated_ref,
    handed_ref,
    *scratch,
):
    terms, width = left_ref.shape[2], left_ref.shape[3]
    count = width // LANES
    group = terms // 4
    parts = (scratch[:count], scratch[count : 2 * count])
    (
        left,
        right,
        turned,
        landed_left,
        half,
        total,
        own,
        combined,
        handed_vector,
        flipped,
        norm_own,
        norm_first,
        norm_row,
        norm_second,
        norm_all,
        norm_landed,
        source_tile,
        source_landed,
        source_before,
        mixing_ref,
        load_sem,
        send_sem,
        recv_sem,
        norm_send,
        norm_recv,
        chain_send,
        chain_recv,
        local_sem,
        out_sem,
        turn_sem,
    ) = scratch[2 * count :]
    chain = lax.axis_index("chain")
    bond = lax.axis_index("bond")
    chains = lax.axis_size("chain")
    z, x = lax.div(bond, RING), lax.rem(bond, RING)
    after = lax.rem(chain + 1, chains)
    before = lax.rem(chain + chains - 1, chains)
    entries = float(RING * RING * width * width)

    load_left = pltpu.make_async_copy(left_ref.at[0, 0], left, load_sem.at[0])
    load_right = pltpu.make_async_copy(right_ref.at[0, 0], right, load_sem.at[1])
    load_left.start()
    load_right.start()
    load_mixing = pltpu.make_async_copy(mixing_hbm, mixing_ref, load_sem.at[2])
    load_mixing.start()

    def along_x(by):
        return z * RING + lax.rem(x + by, RING)

    def along_z(by):
        return lax.rem(z + by, RING) * RING + x

    barrier = pltpu.get_barrier_semaphore()
    for by in range(1, RING):
        for device in (along_x(by), along_z(by)):
            pl.semaphore_signal(barrier, inc=1, device_id={"bond": device}, device_id_type=MESH)
    for device in (after, before):
        pl.semaphore_signal(barrier, inc=1, device_id={"chain": device}, device_id_type=MESH)

    size = sizes_ref[0, 0]
    row_live = lax.broadcasted_iota(jnp.int32, (width, LANES), 0) < size

    def masked(value, part):
        column = lax.broadcasted_iota(jnp.int32, (width, LANES), 1) + part * LANES
        return jnp.where(row_live & (column < size), value, 0.0)

    def columns(part):
        return pl.ds(part * LANES, LANES)

    def tile_sum(value):
        return jnp.sum((value * value).reshape(width // 8, 8, LANES), axis=0)

    gathers = [
        Gather(parts[number % 2], send_sem.at[number % 2], recv_sem.at[number % 2], z, x, width)
        for number in range(PRODUCTS + 1)
    ]

    def to_chain(src, dst, slot):
        return pltpu.make_async_remote_copy(
            src_ref=src,
            dst_ref=dst,
            send_sem=chain_send.at[slot],
            recv_sem=chain_recv.at[slot],
            device_id={"chain": after},
            device_id_type=MESH,
        )

    def norm_copy(number, phase, by):
        return pltpu.make_async_remote_copy(
            src_ref=(norm_own if phase == 0 else norm_row).at[number],
            dst_ref=(norm_first if phase == 0 else norm_second).at[number, by - 1],
            send_sem=norm_send.at[number, phase, by - 1],
            recv_sem=norm_recv.at[number, phase, by - 1],
            device_id={"bond": along_x(by) if phase == 0 else along_z(by)},
            device_id_type=MESH,
        )

    def norm_start(number, tile):
        norm_own[number] = tile
        for by in range(1, RING):
            norm_copy(number, 0, by).start()

    def norm_middle(number):
        for by in range(1, RING):
            norm_copy(number, 0, by).wait_recv()
        norm_row[number] = norm_own[number] + norm_first[number, 0] + norm_first[number, 1] + norm_first[number, 2]
        for by in range(1, RING):
            norm_copy(number, 1, by).start()

    def scale_of(tile):
        summed = jnp.sum(jnp.sum(tile, axis=0, keepdims=True), axis=1, keepdims=True)
        return lax.rsqrt(summed / entries + EPSILON)

    def norm_end(number):
        for by in range(1, RING):
            norm_copy(number, 1, by).wait_recv()
        norm_all[number] = (
            norm_row[number] + norm_second[number, 0] + norm_second[number, 1] + norm_second[number, 2]
        )
        return scale_of(norm_all[number])

    def place(number, part, value):
        own[number, part] = value
        parts[number % 2][part][bond] = value

    values = []
    squares = jnp.zeros((8, LANES), F32)
    for part in range(count):
        value = masked(wave_ref[0, 0, :, columns(part)].astype(F32), part)
        squares = squares + tile_sum(value)
        place(0, part, value.astype(BF16))
    lane = lax.broadcasted_iota(jnp.int32, (8, LANES), 1)
    tile = jnp.zeros((8, LANES), jnp.int32)
    for term in range(terms):
        tile = jnp.where(lane == term, source_ref[0, 0, term], tile)
    source_tile[...] = tile

    pl.semaphore_wait(barrier, 2 * (RING - 1) + 2)
    odd = lax.rem(chain, 2) == 1

    @pl.when(odd)
    def _():
        pl.semaphore_wait(turn_sem, 1)

    gathers[0].stage(0, 0)
    norm_start(0, squares)
    for part in range(1, count):
        gathers[0].stage(0, part)
    send_source = to_chain(source_tile, source_landed, 0)
    send_source.start()
    send_left = to_chain(left_ref.at[0, 0], landed_left, 1)
    send_left.start()

    def turn(number):
        def step(term, carry):
            for part in range(count):
                rows = pl.ds(pl.multiple_of(term * LANES, LANES), LANES)
                turned[part, rows, :] = jnp.transpose(right[term, :, columns(part)])
            return carry

        lax.fori_loop(number * group, (number + 1) * group, step, 0)

    def halves(number, part, which):
        held = parts[number % 2][part]

        for term in range(which * group, (which + 1) * group):
            block = held[source_ref[0, 0, term]]
            product = jnp.dot(left[term], block, preferred_element_type=F32)
            half[:, columns(term)] = product.astype(BF16)

    def gather_sum(part, side):
        wide = pl.ds(side * (width // 2), width // 2)
        product = jnp.dot(half[...], turned[part, :, wide], preferred_element_type=F32)
        if part == 0:
            total[:, wide] = product
        else:
            total[:, wide] += product

    scales = []
    for number in range(PRODUCTS):
        here = gathers[number]
        for item in ORDER:
            if item[0] == "E":
                here.stage(*item[1:])
                if item == EARLY[0]:
                    norm_middle(number)
                if number == 0 and item == TURN:

                    @pl.when(jnp.logical_not(odd))
                    def _():
                        pl.semaphore_signal(turn_sem, inc=1, device_id={"chain": after}, device_id_type=MESH)

                if number == 0 and item in EARLY:
                    if item == EARLY[0]:
                        load_right.wait()
                    turn(EARLY.index(item))
                if number == 0 and item == ("E", 4, 0):
                    load_left.wait()
                    load_mixing.wait()
            elif item[0] == "C":
                halves(number, *item[1:])
            else:
                for side in (0, 1):
                    gather_sum(item[1], side)
        scales.append(norm_end(number))
        for which in range(4):
            halves(number, count - 1, which)
        for part in range(count):
            here.sent(part)
        squares = jnp.zeros((8, LANES), F32)
        for side in (0, 1):
            gather_sum(count - 1, side)
            for part in range(side * count // 2, (side + 1) * count // 2):
                value = scales[number] * masked(total[:, columns(part)], part)
                for other in range(number + 1):
                    factor = mixing_ref[0, number : number + 1, other : other + 1] * scales[other]
                    value = value - factor * own[other, part].astype(F32)
                squares = squares + tile_sum(value)
                if number + 1 < PRODUCTS:
                    place(number + 1, part, value.astype(BF16))
                    gathers[number + 1].stage(0, part)
                else:
                    combined[:, columns(part)] = value
        norm_start(number + 1, squares)

    norm_middle(PRODUCTS)
    last = norm_end(PRODUCTS)
    squares = jnp.zeros((8, LANES), F32)
    for part in range(count):
        value = (weights_ref[0, PRODUCTS] * last) * combined[:, columns(part)]
        for other in range(PRODUCTS):
            value = value + (weights_ref[0, other] * scales[other]) * own[other, part].astype(F32)
        combined[:, columns(part)] = value
        own[PRODUCTS, part] = value.astype(BF16)
        to_chain(own.at[PRODUCTS, part], handed_vector.at[part], 3 + part).start()
        squares = squares + tile_sum(value)
    norm_start(PRODUCTS + 1, squares)

    here = gathers[PRODUCTS]
    for part in range(count):
        to_chain(own.at[PRODUCTS, part], handed_vector.at[part], 3 + part).wait_recv()
        parts[PRODUCTS % 2][part][bond] = handed_vector[part]
        here.stage(0, part)
    norm_middle(PRODUCTS + 1)
    send_source.wait_recv()
    fetch_source = pltpu.make_async_copy(source_landed, source_before, local_sem)
    fetch_source.start()
    for part in range(count):
        flipped[pl.ds(part * LANES, LANES), :] = jnp.transpose(handed_vector[part])
    fetch_source.wait()
    send_left.wait_recv()

    def grow_half(which):
        for term in range(which * group, (which + 1) * group):
            product = jnp.dot(flipped[...], landed_left[term], preferred_element_type=F32)
            right[term] = product.astype(BF16)

    def out_copy(part):
        return pltpu.make_async_copy(
            left.at[:, :, columns(part)], handed_ref.at[0, 0, :, :, columns(part)], out_sem.at[part]
        )

    def grow(part, which, factor):
        held = parts[PRODUCTS % 2][part]

        for term in range(which * group, (which + 1) * group):
            block = held[source_before[0, term]]
            product = jnp.dot(right[term], block, preferred_element_type=F32)
            left[term, :, columns(part)] = (product * factor).astype(BF16)

    factor = None
    for item in ORDER:
        if item[0] == "E":
            here.stage(*item[1:])
            if item in EARLY:
                grow_half(EARLY.index(item))
            if item == EARLY[0]:
                scale = norm_end(PRODUCTS + 1)
                send_norm = to_chain(norm_all.at[PRODUCTS + 1], norm_landed, 2)
                send_norm.start()
                for column in range(count):
                    updated_ref[0, 0, :, columns(column)] = (scale * combined[:, columns(column)]).astype(BF16)
            if item == ("E", 3, 0):
                send_norm.wait_recv()
                scale = scale_of(norm_landed[...])
                factor = scale * scale * (1.0 / math.sqrt(width))
                factor = jnp.where(chain > 0, factor, jnp.zeros_like(factor))
        elif item[0] == "C":
            grow(*item[1:], factor)
        else:
            out_copy(item[1]).start()
    for which in range(4):
        grow(count - 1, which, factor)
    out_copy(count - 1).start()
    for part in range(count):
        here.sent(part)
    for number in range(PRODUCTS + 2):
        for phase in (0, 1):
            for by in range(1, RING):
                norm_copy(number, phase, by).wait_send()
    send_source.wait_send()
    send_left.wait_send()
    send_norm.wait_send()
    for part in range(count):
        to_chain(own.at[PRODUCTS, part], handed_vector.at[part], 3 + part).wait_send()
    for part in range(count):
        out_copy(part).wait()


def body(wavefunction, left_env, right_env, source, block_sizes, davidson_mix, ritz_weights):
    terms, width = left_env.shape[2], left_env.shape[3]
    count = width // LANES
    blocks = (terms, width, width)
    vmem, smem, anywhere = (pl.BlockSpec(memory_space=space) for space in (pltpu.VMEM, pltpu.SMEM, pl.ANY))
    tile = (8, LANES)
    norms = PRODUCTS + 2
    scratch = [pltpu.VMEM((RING * RING, width, LANES), BF16) for _ in range(2 * count)] + [
        pltpu.VMEM(blocks, BF16),
        pltpu.VMEM(blocks, BF16),
        pltpu.VMEM((count, terms * LANES, width), BF16),
        pltpu.VMEM(blocks, BF16),
        pltpu.VMEM((width, terms * LANES), BF16),
        pltpu.VMEM((width, width), F32),
        pltpu.VMEM((PRODUCTS + 1, count, width, LANES), BF16),
        pltpu.VMEM((width, width), F32),
        pltpu.VMEM((count, width, LANES), BF16),
        pltpu.VMEM((width, width), BF16),
        pltpu.VMEM((norms,) + tile, F32),
        pltpu.VMEM((norms, RING - 1) + tile, F32),
        pltpu.VMEM((norms,) + tile, F32),
        pltpu.VMEM((norms, RING - 1) + tile, F32),
        pltpu.VMEM((norms,) + tile, F32),
        pltpu.VMEM(tile, F32),
        pltpu.VMEM(tile, jnp.int32),
        pltpu.VMEM(tile, jnp.int32),
        pltpu.SMEM(tile, jnp.int32),
        pltpu.VMEM(davidson_mix.shape, F32),
        pltpu.SemaphoreType.DMA((3,)),
        pltpu.SemaphoreType.DMA((2, count)),
        pltpu.SemaphoreType.DMA((2, count, 2, 20)),
        pltpu.SemaphoreType.DMA((norms, 2, RING - 1)),
        pltpu.SemaphoreType.DMA((norms, 2, RING - 1)),
        pltpu.SemaphoreType.DMA((3 + count,)),
        pltpu.SemaphoreType.DMA((3 + count,)),
        pltpu.SemaphoreType.DMA,
        pltpu.SemaphoreType.DMA((count,)),
        pltpu.SemaphoreType.REGULAR,
    ]
    flops = (PRODUCTS + 1) * 2 * terms * 2 * width**3
    return pl.pallas_call(
        kernel,
        out_shape=(
            jax.ShapeDtypeStruct(wavefunction.shape, BF16),
            jax.ShapeDtypeStruct(left_env.shape, BF16),
        ),
        in_specs=[vmem, anywhere, anywhere, smem, smem, anywhere, smem],
        out_specs=(vmem, anywhere),
        scratch_shapes=scratch,
        compiler_params=pltpu.CompilerParams(
            collective_id=0, has_side_effects=True, vmem_limit_bytes=60 * 2**20
        ),
        cost_estimate=pl.CostEstimate(flops=flops, bytes_accessed=40 * 2**20, transcendentals=0),
        name="davidson_update",
    )(wavefunction, left_env, right_env, source, block_sizes, davidson_mix, ritz_weights)


def solution(mesh):
    in_specs = (
        P("chain", "bond", None, None),
        P("chain", "bond", None, None, None),
        P("chain", "bond", None, None, None),
        P("chain", "bond", None),
        P("chain", "bond"),
        P("chain", None, None),
        P("chain", None),
    )
    out_specs = (P("chain", "bond", None, None), P("chain", "bond", None, None, None))
    return jax.shard_map(body, mesh=mesh, in_specs=in_specs, out_specs=out_specs, check_vma=False)
```

```python
import math

import jax
import jax.numpy as jnp
from jax import lax
from jax.experimental import pallas as pl
from jax.experimental.pallas import tpu as pltpu
from jax.sharding import PartitionSpec as P

PRODUCTS = 3
EPSILON = 1e-06
MESH = pl.DeviceIdType.MESH
RING = 4
LANES = 128
F32 = jnp.float32
BF16 = jnp.bfloat16

ORDER = (
    (("E", 1, 0), ("E", 1, 1), ("E", 2, 0), ("E", 1, 2), ("E", 3, 0), ("E", 2, 1), ("E", 1, 3), ("E", 4, 0))
    + (("C", 0, 0), ("E", 3, 1), ("C", 0, 1), ("E", 2, 2), ("C", 0, 2), ("E", 4, 1), ("C", 0, 3), ("S", 0))
    + (("E", 3, 2), ("C", 1, 0), ("C", 1, 1), ("E", 2, 3), ("C", 1, 2), ("C", 1, 3), ("S", 1), ("E", 4, 2))
    + (("C", 2, 0), ("E", 3, 3), ("C", 2, 1), ("C", 2, 2), ("C", 2, 3), ("S", 2), ("E", 4, 3))
)
EARLY = (("E", 1, 0), ("E", 1, 1), ("E", 2, 0), ("E", 1, 2))

TURN = ("E", 4, 0)


class Gather:
    def __init__(self, parts, send, recv, z, x, width):
        self.parts, self.send, self.recv = parts, send, recv
        self.z, self.x = z, x
        self.me = z * RING + x
        self.half = width // 2
        self.quarter = width // 4

    def sector(self, path, first, second):
        a, b = (self.x, self.z) if path == 0 else (self.z, self.x)
        a = lax.rem(a + (first + RING), RING)
        b = lax.rem(b + (second + RING), RING)
        return b * RING + a if path == 0 else a * RING + b

    def copy(self, part, path, sector, offset, rows, device, slot):
        ref = self.parts[part].at[sector, pl.ds(path * self.half + offset, rows), :]
        return pltpu.make_async_remote_copy(
            src_ref=ref,
            dst_ref=ref,
            send_sem=self.send.at[part],
            recv_sem=self.recv.at[part, path, slot],
            device_id={"bond": device},
            device_id_type=MESH,
        )

    OFFSETS = (0, 1, -1, 2)

    def own_first(self, part, path):
        for slot, way in ((0, 1), (1, -1)):
            self.copy(part, path, self.me, 0, self.half, self.sector(path, way, 0), slot).start()

    def own_second(self, part, path, which):
        sector = self.sector(path, self.OFFSETS[which], 0)
        for side, way in ((0, 1), (1, -1)):
            slot = 4 + 4 * which + side
            self.copy(part, path, sector, 0, self.half, self.sector(path, 0, way), slot).start()

    def pass_first(self, part, path, side):
        way = 1 if side == 0 else -1
        sector = self.sector(path, -way, 0)
        self.copy(part, path, sector, 0, self.half, self.me, side).wait_recv()
        target = self.sector(path, way, 0)
        self.copy(part, path, sector, self.quarter * side, self.quarter, target, 2 + side).start()

    def end_first(self, part, path):
        sector = self.sector(path, 2, 0)
        for side in (0, 1):
            self.copy(part, path, sector, self.quarter * side, self.quarter, self.me, 2 + side).wait_recv()

    def pass_second(self, part, path, which, side):
        way = 1 if side == 0 else -1
        sector = self.sector(path, self.OFFSETS[which], -way)
        slot = 4 + 4 * which + side
        self.copy(part, path, sector, 0, self.half, self.me, slot).wait_recv()
        target = self.sector(path, 0, way)
        self.copy(part, path, sector, self.quarter * side, self.quarter, target, slot + 2).start()

    def end_second(self, part, path, which):
        sector = self.sector(path, self.OFFSETS[which], 2)
        for side in (0, 1):
            slot = 4 + 4 * which + 2 + side
            self.copy(part, path, sector, self.quarter * side, self.quarter, self.me, slot).wait_recv()

    def stage(self, number, part):
        if number == 0:
            for path in (0, 1):
                self.own_first(part, path)
            for path in (0, 1):
                self.own_second(part, path, 0)
        elif number == 1:
            for side in (0, 1):
                for path in (0, 1):
                    self.pass_first(part, path, side)
                    self.own_second(part, path, 2 if side == 0 else 1)
            for side in (0, 1):
                for path in (0, 1):
                    self.pass_second(part, path, 0, side)
        elif number == 2:
            for path in (0, 1):
                self.end_first(part, path)
                self.own_second(part, path, 3)
            for which in (1, 2):
                for side in (0, 1):
                    for path in (0, 1):
                        self.pass_second(part, path, which, side)
        elif number == 3:
            for side in (0, 1):
                for path in (0, 1):
                    self.pass_second(part, path, 3, side)
        else:
            for path in (0, 1):
                for which in range(4):
                    self.end_second(part, path, which)

    def sent(self, part):
        ref = self.parts[part].at[pl.ds(0, RING * RING - 1)]
        pltpu.make_async_remote_copy(
            src_ref=ref,
            dst_ref=ref,
            send_sem=self.send.at[part],
            recv_sem=self.recv.at[part, 0, 0],
            device_id={"bond": self.me},
            device_id_type=MESH,
        ).wait_send()


def kernel(
    wave_ref,
    left_ref,
    right_ref,
    source_ref,
    sizes_ref,
    mixing_hbm,
    weights_ref,
    updated_ref,
    handed_ref,
    *scratch,
):
    terms, width = left_ref.shape[2], left_ref.shape[3]
    count = width // LANES
    group = terms // 4
    parts = (scratch[:count], scratch[count : 2 * count])
    (
        left,
        right,
        turned,
        landed_left,
        half,
        total,
        own,
        combined,
        handed_vector,
        flipped,
        norm_own,
        norm_first,
        norm_row,
        norm_second,
        norm_all,
        norm_landed,
        source_tile,
        source_landed,
        source_before,
        mixing_ref,
        load_sem,
        send_sem,
        recv_sem,
        norm_send,
        norm_recv,
        chain_send,
        chain_recv,
        local_sem,
        out_sem,
        turn_sem,
    ) = scratch[2 * count :]
    chain = lax.axis_index("chain")
    bond = lax.axis_index("bond")
    chains = lax.axis_size("chain")
    z, x = lax.div(bond, RING), lax.rem(bond, RING)
    after = lax.rem(chain + 1, chains)
    before = lax.rem(chain + chains - 1, chains)
    entries = float(RING * RING * width * width)

    load_left = pltpu.make_async_copy(left_ref.at[0, 0], left, load_sem.at[0])
    load_right = pltpu.make_async_copy(right_ref.at[0, 0], right, load_sem.at[1])
    load_left.start()
    load_right.start()
    load_mixing = pltpu.make_async_copy(mixing_hbm, mixing_ref, load_sem.at[2])
    load_mixing.start()

    def along_x(by):
        return z * RING + lax.rem(x + by, RING)

    def along_z(by):
        return lax.rem(z + by, RING) * RING + x

    barrier = pltpu.get_barrier_semaphore()
    for by in range(1, RING):
        for device in (along_x(by), along_z(by)):
            pl.semaphore_signal(barrier, inc=1, device_id={"bond": device}, device_id_type=MESH)
    for device in (after, before):
        pl.semaphore_signal(barrier, inc=1, device_id={"chain": device}, device_id_type=MESH)

    size = sizes_ref[0, 0]
    row_live = lax.broadcasted_iota(jnp.int32, (width, LANES), 0) < size

    def masked(value, part):
        column = lax.broadcasted_iota(jnp.int32, (width, LANES), 1) + part * LANES
        return jnp.where(row_live & (column < size), value, 0.0)

    def columns(part):
        return pl.ds(part * LANES, LANES)

    def tile_sum(value):
        return jnp.sum((value * value).reshape(width // 8, 8, LANES), axis=0)

    gathers = [
        Gather(parts[number % 2], send_sem.at[number % 2], recv_sem.at[number % 2], z, x, width)
        for number in range(PRODUCTS + 1)
    ]

    def to_chain(src, dst, slot):
        return pltpu.make_async_remote_copy(
            src_ref=src,
            dst_ref=dst,
            send_sem=chain_send.at[slot],
            recv_sem=chain_recv.at[slot],
            device_id={"chain": after},
            device_id_type=MESH,
        )

    def norm_copy(number, phase, by):
        return pltpu.make_async_remote_copy(
            src_ref=(norm_own if phase == 0 else norm_row).at[number],
            dst_ref=(norm_first if phase == 0 else norm_second).at[number, by - 1],
            send_sem=norm_send.at[number, phase, by - 1],
            recv_sem=norm_recv.at[number, phase, by - 1],
            device_id={"bond": along_x(by) if phase == 0 else along_z(by)},
            device_id_type=MESH,
        )

    def norm_start(number, tile):
        norm_own[number] = tile
        for by in range(1, RING):
            norm_copy(number, 0, by).start()

    def norm_middle(number):
        for by in range(1, RING):
            norm_copy(number, 0, by).wait_recv()
        norm_row[number] = norm_own[number] + norm_first[number, 0] + norm_first[number, 1] + norm_first[number, 2]
        for by in range(1, RING):
            norm_copy(number, 1, by).start()

    def scale_of(tile):
        summed = jnp.sum(jnp.sum(tile, axis=0, keepdims=True), axis=1, keepdims=True)
        return lax.rsqrt(summed / entries + EPSILON)

    def norm_end(number):
        for by in range(1, RING):
            norm_copy(number, 1, by).wait_recv()
        norm_all[number] = (
            norm_row[number] + norm_second[number, 0] + norm_second[number, 1] + norm_second[number, 2]
        )
        return scale_of(norm_all[number])

    def place(number, part, value):
        own[number, part] = value
        parts[number % 2][part][bond] = value

    values = []
    squares = jnp.zeros((8, LANES), F32)
    for part in range(count):
        value = masked(wave_ref[0, 0, :, columns(part)].astype(F32), part)
        squares = squares + tile_sum(value)
        place(0, part, value.astype(BF16))
    lane = lax.broadcasted_iota(jnp.int32, (8, LANES), 1)
    tile = jnp.zeros((8, LANES), jnp.int32)
    for term in range(terms):
        tile = jnp.where(lane == term, source_ref[0, 0, term], tile)
    source_tile[...] = tile

    pl.semaphore_wait(barrier, 2 * (RING - 1) + 2)
    odd = lax.rem(chain, 2) == 1

    @pl.when(odd)
    def _():
        pl.semaphore_wait(turn_sem, 1)

    gathers[0].stage(0, 0)
    norm_start(0, squares)
    for part in range(1, count):
        gathers[0].stage(0, part)
    send_source = to_chain(source_tile, source_landed, 0)
    send_source.start()
    send_left = to_chain(left_ref.at[0, 0], landed_left, 1)
    send_left.start()

    def turn(number):
        def step(term, carry):
            for part in range(count):
                rows = pl.ds(pl.multiple_of(term * LANES, LANES), LANES)
                turned[part, rows, :] = jnp.transpose(right[term, :, columns(part)])
            return carry

        lax.fori_loop(number * group, (number + 1) * group, step, 0)

    def halves(number, part, which):
        held = parts[number % 2][part]

        def step(term, carry):
            block = held[source_ref[0, 0, term]]
            product = jnp.dot(left[term], block, preferred_element_type=F32)
            half[:, pl.ds(pl.multiple_of(term * LANES, LANES), LANES)] = product.astype(BF16)
            return carry

        lax.fori_loop(which * group, (which + 1) * group, step, 0, unroll=part == count - 1)

    def gather_sum(part, side):
        wide = pl.ds(side * (width // 2), width // 2)
        product = jnp.dot(half[...], turned[part, :, wide], preferred_element_type=F32)
        if part == 0:
            total[:, wide] = product
        else:
            total[:, wide] += product

    scales = []
    for number in range(PRODUCTS):
        here = gathers[number]
        for item in ORDER:
            if item[0] == "E":
                here.stage(*item[1:])
                if item == EARLY[0]:
                    norm_middle(number)
                if number == 0 and item == TURN:

                    @pl.when(jnp.logical_not(odd))
                    def _():
                        pl.semaphore_signal(turn_sem, inc=1, device_id={"chain": after}, device_id_type=MESH)

                if number == 0 and item in EARLY:
                    if item == EARLY[0]:
                        load_right.wait()
                    turn(EARLY.index(item))
                if number == 0 and item == ("E", 4, 0):
                    load_left.wait()
                    load_mixing.wait()
            elif item[0] == "C":
                halves(number, *item[1:])
            else:
                for side in (0, 1):
                    gather_sum(item[1], side)
        scales.append(norm_end(number))
        for which in range(4):
            halves(number, count - 1, which)
        for part in range(count):
            here.sent(part)
        squares = jnp.zeros((8, LANES), F32)
        for side in (0, 1):
            gather_sum(count - 1, side)
            for part in range(side * count // 2, (side + 1) * count // 2):
                value = scales[number] * masked(total[:, columns(part)], part)
                for other in range(number + 1):
                    factor = mixing_ref[0, number : number + 1, other : other + 1] * scales[other]
                    value = value - factor * own[other, part].astype(F32)
                squares = squares + tile_sum(value)
                if number + 1 < PRODUCTS:
                    place(number + 1, part, value.astype(BF16))
                    gathers[number + 1].stage(0, part)
                else:
                    combined[:, columns(part)] = value
        norm_start(number + 1, squares)

    norm_middle(PRODUCTS)
    last = norm_end(PRODUCTS)
    squares = jnp.zeros((8, LANES), F32)
    for part in range(count):
        value = (weights_ref[0, PRODUCTS] * last) * combined[:, columns(part)]
        for other in range(PRODUCTS):
            value = value + (weights_ref[0, other] * scales[other]) * own[other, part].astype(F32)
        combined[:, columns(part)] = value
        own[PRODUCTS, part] = value.astype(BF16)
        to_chain(own.at[PRODUCTS, part], handed_vector.at[part], 3 + part).start()
        squares = squares + tile_sum(value)
    norm_start(PRODUCTS + 1, squares)

    here = gathers[PRODUCTS]
    for part in range(count):
        to_chain(own.at[PRODUCTS, part], handed_vector.at[part], 3 + part).wait_recv()
        parts[PRODUCTS % 2][part][bond] = handed_vector[part]
        here.stage(0, part)
    norm_middle(PRODUCTS + 1)
    send_source.wait_recv()
    fetch_source = pltpu.make_async_copy(source_landed, source_before, local_sem)
    fetch_source.start()
    for part in range(count):
        flipped[pl.ds(part * LANES, LANES), :] = jnp.transpose(handed_vector[part])
    fetch_source.wait()
    send_left.wait_recv()

    def grow_half(which):
        def step(term, carry):
            product = jnp.dot(flipped[...], landed_left[term], preferred_element_type=F32)
            right[term] = product.astype(BF16)
            return carry

        lax.fori_loop(which * group, (which + 1) * group, step, 0)

    def out_copy(part):
        return pltpu.make_async_copy(
            left.at[:, :, columns(part)], handed_ref.at[0, 0, :, :, columns(part)], out_sem.at[part]
        )

    def grow(part, which, factor):
        held = parts[PRODUCTS % 2][part]

        def step(term, carry):
            block = held[source_before[0, term]]
            product = jnp.dot(right[term], block, preferred_element_type=F32)
            left[term, :, columns(part)] = (product * factor).astype(BF16)
            return carry

        lax.fori_loop(which * group, (which + 1) * group, step, 0, unroll=part == count - 1)

    factor = None
    for item in ORDER:
        if item[0] == "E":
            here.stage(*item[1:])
            if item in EARLY:
                grow_half(EARLY.index(item))
            if item == EARLY[0]:
                scale = norm_end(PRODUCTS + 1)
                send_norm = to_chain(norm_all.at[PRODUCTS + 1], norm_landed, 2)
                send_norm.start()
                for column in range(count):
                    updated_ref[0, 0, :, columns(column)] = (scale * combined[:, columns(column)]).astype(BF16)
            if item == ("E", 3, 0):
                send_norm.wait_recv()
                scale = scale_of(norm_landed[...])
                factor = scale * scale * (1.0 / math.sqrt(width))
                factor = jnp.where(chain > 0, factor, jnp.zeros_like(factor))
        elif item[0] == "C":
            grow(*item[1:], factor)
        else:
            out_copy(item[1]).start()
    for which in range(4):
        grow(count - 1, which, factor)
    out_copy(count - 1).start()
    for part in range(count):
        here.sent(part)
    for number in range(PRODUCTS + 2):
        for phase in (0, 1):
            for by in range(1, RING):
                norm_copy(number, phase, by).wait_send()
    send_source.wait_send()
    send_left.wait_send()
    send_norm.wait_send()
    for part in range(count):
        to_chain(own.at[PRODUCTS, part], handed_vector.at[part], 3 + part).wait_send()
    for part in range(count):
        out_copy(part).wait()


def keep_kernel(updated_ref, handed_ref, updated_out, handed_out, rest, rest_updated, load, store):
    loads = [pltpu.make_async_copy(updated_ref, rest_updated, load.at[0])]
    stores = [pltpu.make_async_copy(rest_updated, updated_out, store.at[0])]
    for term in range(handed_ref.shape[2]):
        loads.append(pltpu.make_async_copy(handed_ref.at[0, 0, term], rest.at[term], load.at[term + 1]))
        stores.append(pltpu.make_async_copy(rest.at[term], handed_out.at[0, 0, term], store.at[term + 1]))
    for copy in loads:
        copy.start()
    for first, second in zip(loads, stores):
        first.wait()
        second.start()
    for copy in stores:
        copy.wait()


def keep(updated, handed):
    anywhere = pl.BlockSpec(memory_space=pl.ANY)
    copies = handed.shape[2] + 1
    return pl.pallas_call(
        keep_kernel,
        out_shape=(
            jax.ShapeDtypeStruct(updated.shape, BF16),
            jax.ShapeDtypeStruct(handed.shape, BF16),
        ),
        in_specs=[anywhere, anywhere],
        out_specs=(anywhere, anywhere),
        scratch_shapes=[
            pltpu.VMEM(handed.shape[2:], BF16),
            pltpu.VMEM(updated.shape, BF16),
            pltpu.SemaphoreType.DMA((copies,)),
            pltpu.SemaphoreType.DMA((copies,)),
        ],
        compiler_params=pltpu.CompilerParams(vmem_limit_bytes=60 * 2**20),
        name="keep",
    )(updated, handed)


def body(wavefunction, left_env, right_env, source, block_sizes, davidson_mix, ritz_weights):
    terms, width = left_env.shape[2], left_env.shape[3]
    count = width // LANES
    blocks = (terms, width, width)
    vmem, smem, anywhere = (pl.BlockSpec(memory_space=space) for space in (pltpu.VMEM, pltpu.SMEM, pl.ANY))
    tile = (8, LANES)
    norms = PRODUCTS + 2
    scratch = [pltpu.VMEM((RING * RING, width, LANES), BF16) for _ in range(2 * count)] + [
        pltpu.VMEM(blocks, BF16),
        pltpu.VMEM(blocks, BF16),
        pltpu.VMEM((count, terms * LANES, width), BF16),
        pltpu.VMEM(blocks, BF16),
        pltpu.VMEM((width, terms * LANES), BF16),
        pltpu.VMEM((width, width), F32),
        pltpu.VMEM((PRODUCTS + 1, count, width, LANES), BF16),
        pltpu.VMEM((width, width), F32),
        pltpu.VMEM((count, width, LANES), BF16),
        pltpu.VMEM((width, width), BF16),
        pltpu.VMEM((norms,) + tile, F32),
        pltpu.VMEM((norms, RING - 1) + tile, F32),
        pltpu.VMEM((norms,) + tile, F32),
        pltpu.VMEM((norms, RING - 1) + tile, F32),
        pltpu.VMEM((norms,) + tile, F32),
        pltpu.VMEM(tile, F32),
        pltpu.VMEM(tile, jnp.int32),
        pltpu.VMEM(tile, jnp.int32),
        pltpu.SMEM(tile, jnp.int32),
        pltpu.VMEM(davidson_mix.shape, F32),
        pltpu.SemaphoreType.DMA((3,)),
        pltpu.SemaphoreType.DMA((2, count)),
        pltpu.SemaphoreType.DMA((2, count, 2, 20)),
        pltpu.SemaphoreType.DMA((norms, 2, RING - 1)),
        pltpu.SemaphoreType.DMA((norms, 2, RING - 1)),
        pltpu.SemaphoreType.DMA((3 + count,)),
        pltpu.SemaphoreType.DMA((3 + count,)),
        pltpu.SemaphoreType.DMA,
        pltpu.SemaphoreType.DMA((count,)),
        pltpu.SemaphoreType.REGULAR,
    ]
    flops = (PRODUCTS + 1) * 2 * terms * 2 * width**3
    updated, handed = pl.pallas_call(
        kernel,
        out_shape=(
            jax.ShapeDtypeStruct(wavefunction.shape, BF16),
            jax.ShapeDtypeStruct(left_env.shape, BF16),
        ),
        in_specs=[vmem, anywhere, anywhere, smem, smem, anywhere, smem],
        out_specs=(vmem, anywhere),
        scratch_shapes=scratch,
        compiler_params=pltpu.CompilerParams(
            collective_id=0, has_side_effects=True, vmem_limit_bytes=60 * 2**20
        ),
        cost_estimate=pl.CostEstimate(flops=flops, bytes_accessed=40 * 2**20, transcendentals=0),
        name="davidson_update",
    )(wavefunction, left_env, right_env, source, block_sizes, davidson_mix, ritz_weights)
    return keep(updated, handed)


def solution(mesh):
    in_specs = (
        P("chain", "bond", None, None),
        P("chain", "bond", None, None, None),
        P("chain", "bond", None, None, None),
        P("chain", "bond", None),
        P("chain", "bond"),
        P("chain", None, None),
        P("chain", None),
    )
    out_specs = (P("chain", "bond", None, None), P("chain", "bond", None, None, None))
    return jax.shard_map(body, mesh=mesh, in_specs=in_specs, out_specs=out_specs, check_vma=False)
```

```python
import math

import jax
import jax.numpy as jnp
from jax import lax
from jax.experimental import pallas as pl
from jax.experimental.pallas import tpu as pltpu
from jax.sharding import PartitionSpec as P

PRODUCTS = 3
EPSILON = 1e-06
MESH = pl.DeviceIdType.MESH
RING = 4
LANES = 128
F32 = jnp.float32
BF16 = jnp.bfloat16

ORDER = (
    (("E", 1, 0), ("E", 1, 1), ("E", 2, 0), ("E", 1, 2), ("E", 3, 0), ("E", 2, 1), ("E", 1, 3), ("E", 4, 0))
    + (("C", 0, 0), ("E", 3, 1), ("C", 0, 1), ("E", 2, 2), ("C", 0, 2), ("E", 4, 1), ("S", 0))
    + (("E", 3, 2), ("C", 1, 0), ("E", 2, 3), ("C", 1, 1), ("C", 1, 2), ("S", 1), ("E", 4, 2))
    + (("C", 2, 0), ("E", 3, 3), ("C", 2, 1), ("C", 2, 2), ("S", 2), ("E", 4, 3))
)
GROUPS = 3
EARLY = (("E", 1, 0), ("E", 1, 1), ("E", 2, 0), ("E", 1, 2))

TURN = ("E", 4, 0)


class Gather:
    def __init__(self, parts, send, recv, z, x, width):
        self.parts, self.send, self.recv = parts, send, recv
        self.z, self.x = z, x
        self.me = z * RING + x
        self.half = width // 2
        self.quarter = width // 4

    def sector(self, path, first, second):
        a, b = (self.x, self.z) if path == 0 else (self.z, self.x)
        a = lax.rem(a + (first + RING), RING)
        b = lax.rem(b + (second + RING), RING)
        return b * RING + a if path == 0 else a * RING + b

    def copy(self, part, path, sector, offset, rows, device, slot):
        ref = self.parts[part].at[sector, pl.ds(path * self.half + offset, rows), :]
        return pltpu.make_async_remote_copy(
            src_ref=ref,
            dst_ref=ref,
            send_sem=self.send.at[part],
            recv_sem=self.recv.at[part, path, slot],
            device_id={"bond": device},
            device_id_type=MESH,
        )

    OFFSETS = (0, 1, -1, 2)

    def own_first(self, part, path):
        for slot, way in ((0, 1), (1, -1)):
            self.copy(part, path, self.me, 0, self.half, self.sector(path, way, 0), slot).start()

    def own_second(self, part, path, which):
        sector = self.sector(path, self.OFFSETS[which], 0)
        for side, way in ((0, 1), (1, -1)):
            slot = 4 + 4 * which + side
            self.copy(part, path, sector, 0, self.half, self.sector(path, 0, way), slot).start()

    def pass_first(self, part, path, side):
        way = 1 if side == 0 else -1
        sector = self.sector(path, -way, 0)
        self.copy(part, path, sector, 0, self.half, self.me, side).wait_recv()
        target = self.sector(path, way, 0)
        self.copy(part, path, sector, self.quarter * side, self.quarter, target, 2 + side).start()

    def end_first(self, part, path):
        sector = self.sector(path, 2, 0)
        for side in (0, 1):
            self.copy(part, path, sector, self.quarter * side, self.quarter, self.me, 2 + side).wait_recv()

    def pass_second(self, part, path, which, side):
        way = 1 if side == 0 else -1
        sector = self.sector(path, self.OFFSETS[which], -way)
        slot = 4 + 4 * which + side
        self.copy(part, path, sector, 0, self.half, self.me, slot).wait_recv()
        target = self.sector(path, 0, way)
        self.copy(part, path, sector, self.quarter * side, self.quarter, target, slot + 2).start()

    def end_second(self, part, path, which):
        sector = self.sector(path, self.OFFSETS[which], 2)
        for side in (0, 1):
            slot = 4 + 4 * which + 2 + side
            self.copy(part, path, sector, self.quarter * side, self.quarter, self.me, slot).wait_recv()

    def stage(self, number, part):
        if number == 0:
            for path in (0, 1):
                self.own_first(part, path)
            for path in (0, 1):
                self.own_second(part, path, 0)
        elif number == 1:
            for side in (0, 1):
                for path in (0, 1):
                    self.pass_first(part, path, side)
                    self.own_second(part, path, 2 if side == 0 else 1)
            for side in (0, 1):
                for path in (0, 1):
                    self.pass_second(part, path, 0, side)
        elif number == 2:
            for path in (0, 1):
                self.end_first(part, path)
                self.own_second(part, path, 3)
            for which in (1, 2):
                for side in (0, 1):
                    for path in (0, 1):
                        self.pass_second(part, path, which, side)
        elif number == 3:
            for side in (0, 1):
                for path in (0, 1):
                    self.pass_second(part, path, 3, side)
        else:
            for path in (0, 1):
                for which in range(4):
                    self.end_second(part, path, which)

    def sent(self, part):
        ref = self.parts[part].at[pl.ds(0, RING * RING - 1)]
        pltpu.make_async_remote_copy(
            src_ref=ref,
            dst_ref=ref,
            send_sem=self.send.at[part],
            recv_sem=self.recv.at[part, 0, 0],
            device_id={"bond": self.me},
            device_id_type=MESH,
        ).wait_send()


def kernel(
    wave_ref,
    left_ref,
    right_ref,
    source_ref,
    sizes_ref,
    mixing_hbm,
    weights_ref,
    updated_ref,
    handed_ref,
    *scratch,
):
    terms, width = left_ref.shape[2], left_ref.shape[3]
    count = width // LANES
    group = terms // GROUPS
    share = terms // len(EARLY)
    parts = (scratch[:count], scratch[count : 2 * count])
    (
        left,
        right,
        turned,
        landed_left,
        half,
        total,
        own,
        combined,
        handed_vector,
        flipped,
        norm_own,
        norm_first,
        norm_row,
        norm_second,
        norm_all,
        norm_landed,
        source_tile,
        source_landed,
        source_before,
        mixing_ref,
        load_sem,
        send_sem,
        recv_sem,
        norm_send,
        norm_recv,
        chain_send,
        chain_recv,
        local_sem,
        out_sem,
        turn_sem,
    ) = scratch[2 * count :]
    chain = lax.axis_index("chain")
    bond = lax.axis_index("bond")
    chains = lax.axis_size("chain")
    z, x = lax.div(bond, RING), lax.rem(bond, RING)
    after = lax.rem(chain + 1, chains)
    before = lax.rem(chain + chains - 1, chains)
    entries = float(RING * RING * width * width)

    load_left = pltpu.make_async_copy(left_ref.at[0, 0], left, load_sem.at[0])
    load_right = pltpu.make_async_copy(right_ref.at[0, 0], right, load_sem.at[1])
    load_left.start()
    load_right.start()
    load_mixing = pltpu.make_async_copy(mixing_hbm, mixing_ref, load_sem.at[2])
    load_mixing.start()

    def along_x(by):
        return z * RING + lax.rem(x + by, RING)

    def along_z(by):
        return lax.rem(z + by, RING) * RING + x

    barrier = pltpu.get_barrier_semaphore()
    for by in range(1, RING):
        for device in (along_x(by), along_z(by)):
            pl.semaphore_signal(barrier, inc=1, device_id={"bond": device}, device_id_type=MESH)
    for device in (after, before):
        pl.semaphore_signal(barrier, inc=1, device_id={"chain": device}, device_id_type=MESH)

    size = sizes_ref[0, 0]
    row_live = lax.broadcasted_iota(jnp.int32, (width, LANES), 0) < size

    def masked(value, part):
        column = lax.broadcasted_iota(jnp.int32, (width, LANES), 1) + part * LANES
        return jnp.where(row_live & (column < size), value, 0.0)

    def columns(part):
        return pl.ds(part * LANES, LANES)

    def tile_sum(value):
        return jnp.sum((value * value).reshape(width // 8, 8, LANES), axis=0)

    gathers = [
        Gather(parts[number % 2], send_sem.at[number % 2], recv_sem.at[number % 2], z, x, width)
        for number in range(PRODUCTS + 1)
    ]

    def to_chain(src, dst, slot):
        return pltpu.make_async_remote_copy(
            src_ref=src,
            dst_ref=dst,
            send_sem=chain_send.at[slot],
            recv_sem=chain_recv.at[slot],
            device_id={"chain": after},
            device_id_type=MESH,
        )

    def norm_copy(number, phase, by):
        return pltpu.make_async_remote_copy(
            src_ref=(norm_own if phase == 0 else norm_row).at[number],
            dst_ref=(norm_first if phase == 0 else norm_second).at[number, by - 1],
            send_sem=norm_send.at[number, phase, by - 1],
            recv_sem=norm_recv.at[number, phase, by - 1],
            device_id={"bond": along_x(by) if phase == 0 else along_z(by)},
            device_id_type=MESH,
        )

    def norm_start(number, tile):
        norm_own[number] = tile
        for by in range(1, RING):
            norm_copy(number, 0, by).start()

    def norm_middle(number):
        for by in range(1, RING):
            norm_copy(number, 0, by).wait_recv()
        norm_row[number] = norm_own[number] + norm_first[number, 0] + norm_first[number, 1] + norm_first[number, 2]
        for by in range(1, RING):
            norm_copy(number, 1, by).start()

    def scale_of(tile):
        summed = jnp.sum(jnp.sum(tile, axis=0, keepdims=True), axis=1, keepdims=True)
        return lax.rsqrt(summed / entries + EPSILON)

    def norm_end(number):
        for by in range(1, RING):
            norm_copy(number, 1, by).wait_recv()
        norm_all[number] = (
            norm_row[number] + norm_second[number, 0] + norm_second[number, 1] + norm_second[number, 2]
        )
        return scale_of(norm_all[number])

    def place(number, part, value):
        own[number, part] = value
        parts[number % 2][part][bond] = value

    values = []
    squares = jnp.zeros((8, LANES), F32)
    for part in range(count):
        value = masked(wave_ref[0, 0, :, columns(part)].astype(F32), part)
        squares = squares + tile_sum(value)
        place(0, part, value.astype(BF16))
    lane = lax.broadcasted_iota(jnp.int32, (8, LANES), 1)
    tile = jnp.zeros((8, LANES), jnp.int32)
    for term in range(terms):
        tile = jnp.where(lane == term, source_ref[0, 0, term], tile)
    source_tile[...] = tile

    pl.semaphore_wait(barrier, 2 * (RING - 1) + 2)
    odd = lax.rem(chain, 2) == 1

    @pl.when(odd)
    def _():
        pl.semaphore_wait(turn_sem, 1)

    gathers[0].stage(0, 0)
    norm_start(0, squares)
    for part in range(1, count):
        gathers[0].stage(0, part)
    send_source = to_chain(source_tile, source_landed, 0)
    send_source.start()
    send_left = to_chain(left_ref.at[0, 0], landed_left, 1)
    send_left.start()

    def turn(number):
        def step(term, carry):
            for part in range(count):
                rows = pl.ds(pl.multiple_of(term * LANES, LANES), LANES)
                turned[part, rows, :] = jnp.transpose(right[term, :, columns(part)])
            return carry

        lax.fori_loop(number * share, (number + 1) * share, step, 0)

    def halves(number, part, which):
        held = parts[number % 2][part]

        def step(term, carry):
            block = held[source_ref[0, 0, term]]
            product = jnp.dot(left[term], block, preferred_element_type=F32)
            half[:, pl.ds(pl.multiple_of(term * LANES, LANES), LANES)] = product.astype(BF16)
            return carry

        lax.fori_loop(which * group, (which + 1) * group, step, 0, unroll=group if part == count - 1 else 2)

    def gather_sum(part, side):
        wide = pl.ds(side * (width // 2), width // 2)
        product = jnp.dot(half[...], turned[part, :, wide], preferred_element_type=F32)
        if part == 0:
            total[:, wide] = product
        else:
            total[:, wide] += product

    scales = []
    for number in range(PRODUCTS):
        here = gathers[number]
        for item in ORDER:
            if item[0] == "E":
                here.stage(*item[1:])
                if item == EARLY[0]:
                    norm_middle(number)
                if number == 0 and item == TURN:

                    @pl.when(jnp.logical_not(odd))
                    def _():
                        pl.semaphore_signal(turn_sem, inc=1, device_id={"chain": after}, device_id_type=MESH)

                if number == 0 and item in EARLY:
                    if item == EARLY[0]:
                        load_right.wait()
                    turn(EARLY.index(item))
                if number == 0 and item == ("E", 4, 0):
                    load_left.wait()
                    load_mixing.wait()
            elif item[0] == "C":
                halves(number, *item[1:])
            else:
                for side in (0, 1):
                    gather_sum(item[1], side)
        scales.append(norm_end(number))
        for which in range(GROUPS):
            halves(number, count - 1, which)
        for part in range(count):
            here.sent(part)
        squares = jnp.zeros((8, LANES), F32)
        for side in (0, 1):
            gather_sum(count - 1, side)
            for part in range(side * count // 2, (side + 1) * count // 2):
                value = scales[number] * masked(total[:, columns(part)], part)
                for other in range(number + 1):
                    factor = mixing_ref[0, number : number + 1, other : other + 1] * scales[other]
                    value = value - factor * own[other, part].astype(F32)
                squares = squares + tile_sum(value)
                if number + 1 < PRODUCTS:
                    place(number + 1, part, value.astype(BF16))
                    gathers[number + 1].stage(0, part)
                else:
                    combined[:, columns(part)] = value
        norm_start(number + 1, squares)

    norm_middle(PRODUCTS)
    last = norm_end(PRODUCTS)
    squares = jnp.zeros((8, LANES), F32)
    for part in range(count):
        value = (weights_ref[0, PRODUCTS] * last) * combined[:, columns(part)]
        for other in range(PRODUCTS):
            value = value + (weights_ref[0, other] * scales[other]) * own[other, part].astype(F32)
        combined[:, columns(part)] = value
        own[PRODUCTS, part] = value.astype(BF16)
        to_chain(own.at[PRODUCTS, part], handed_vector.at[part], 3 + part).start()
        squares = squares + tile_sum(value)
    norm_start(PRODUCTS + 1, squares)

    here = gathers[PRODUCTS]
    for part in range(count):
        to_chain(own.at[PRODUCTS, part], handed_vector.at[part], 3 + part).wait_recv()
        parts[PRODUCTS % 2][part][bond] = handed_vector[part]
        here.stage(0, part)
    norm_middle(PRODUCTS + 1)
    send_source.wait_recv()
    fetch_source = pltpu.make_async_copy(source_landed, source_before, local_sem)
    fetch_source.start()
    for part in range(count):
        flipped[pl.ds(part * LANES, LANES), :] = jnp.transpose(handed_vector[part])
    fetch_source.wait()
    send_left.wait_recv()

    def grow_half(which):
        def step(term, carry):
            product = jnp.dot(flipped[...], landed_left[term], preferred_element_type=F32)
            right[term] = product.astype(BF16)
            return carry

        lax.fori_loop(which * share, (which + 1) * share, step, 0)

    def out_copy(part):
        return pltpu.make_async_copy(
            left.at[:, :, columns(part)], handed_ref.at[0, 0, :, :, columns(part)], out_sem.at[part]
        )

    def grow(part, which, factor):
        held = parts[PRODUCTS % 2][part]

        def step(term, carry):
            block = held[source_before[0, term]]
            product = jnp.dot(right[term], block, preferred_element_type=F32)
            left[term, :, columns(part)] = (product * factor).astype(BF16)
            return carry

        lax.fori_loop(which * group, (which + 1) * group, step, 0, unroll=group if part == count - 1 else 2)

    factor = None
    for item in ORDER:
        if item[0] == "E":
            here.stage(*item[1:])
            if item in EARLY:
                grow_half(EARLY.index(item))
            if item == EARLY[0]:
                scale = norm_end(PRODUCTS + 1)
                send_norm = to_chain(norm_all.at[PRODUCTS + 1], norm_landed, 2)
                send_norm.start()
                for column in range(count):
                    updated_ref[0, 0, :, columns(column)] = (scale * combined[:, columns(column)]).astype(BF16)
            if item == ("E", 3, 0):
                send_norm.wait_recv()
                scale = scale_of(norm_landed[...])
                factor = scale * scale * (1.0 / math.sqrt(width))
                factor = jnp.where(chain > 0, factor, jnp.zeros_like(factor))
        elif item[0] == "C":
            grow(*item[1:], factor)
        else:
            out_copy(item[1]).start()
    for which in range(GROUPS):
        grow(count - 1, which, factor)
    out_copy(count - 1).start()
    for part in range(count):
        here.sent(part)
    for number in range(PRODUCTS + 2):
        for phase in (0, 1):
            for by in range(1, RING):
                norm_copy(number, phase, by).wait_send()
    send_source.wait_send()
    send_left.wait_send()
    send_norm.wait_send()
    for part in range(count):
        to_chain(own.at[PRODUCTS, part], handed_vector.at[part], 3 + part).wait_send()
    for part in range(count):
        out_copy(part).wait()


def keep_kernel(updated_ref, handed_ref, updated_out, handed_out, rest, rest_updated, load, store):
    loads = [pltpu.make_async_copy(updated_ref, rest_updated, load.at[0])]
    stores = [pltpu.make_async_copy(rest_updated, updated_out, store.at[0])]
    for term in range(handed_ref.shape[2]):
        loads.append(pltpu.make_async_copy(handed_ref.at[0, 0, term], rest.at[term], load.at[term + 1]))
        stores.append(pltpu.make_async_copy(rest.at[term], handed_out.at[0, 0, term], store.at[term + 1]))
    for copy in loads:
        copy.start()
    for first, second in zip(loads, stores):
        first.wait()
        second.start()
    for copy in stores:
        copy.wait()


def keep(updated, handed):
    anywhere = pl.BlockSpec(memory_space=pl.ANY)
    copies = handed.shape[2] + 1
    return pl.pallas_call(
        keep_kernel,
        out_shape=(
            jax.ShapeDtypeStruct(updated.shape, BF16),
            jax.ShapeDtypeStruct(handed.shape, BF16),
        ),
        in_specs=[anywhere, anywhere],
        out_specs=(anywhere, anywhere),
        scratch_shapes=[
            pltpu.VMEM(handed.shape[2:], BF16),
            pltpu.VMEM(updated.shape, BF16),
            pltpu.SemaphoreType.DMA((copies,)),
            pltpu.SemaphoreType.DMA((copies,)),
        ],
        compiler_params=pltpu.CompilerParams(vmem_limit_bytes=60 * 2**20),
        name="keep",
    )(updated, handed)


def body(wavefunction, left_env, right_env, source, block_sizes, davidson_mix, ritz_weights):
    terms, width = left_env.shape[2], left_env.shape[3]
    count = width // LANES
    blocks = (terms, width, width)
    vmem, smem, anywhere = (pl.BlockSpec(memory_space=space) for space in (pltpu.VMEM, pltpu.SMEM, pl.ANY))
    tile = (8, LANES)
    norms = PRODUCTS + 2
    scratch = [pltpu.VMEM((RING * RING, width, LANES), BF16) for _ in range(2 * count)] + [
        pltpu.VMEM(blocks, BF16),
        pltpu.VMEM(blocks, BF16),
        pltpu.VMEM((count, terms * LANES, width), BF16),
        pltpu.VMEM(blocks, BF16),
        pltpu.VMEM((width, terms * LANES), BF16),
        pltpu.VMEM((width, width), F32),
        pltpu.VMEM((PRODUCTS + 1, count, width, LANES), BF16),
        pltpu.VMEM((width, width), F32),
        pltpu.VMEM((count, width, LANES), BF16),
        pltpu.VMEM((width, width), BF16),
        pltpu.VMEM((norms,) + tile, F32),
        pltpu.VMEM((norms, RING - 1) + tile, F32),
        pltpu.VMEM((norms,) + tile, F32),
        pltpu.VMEM((norms, RING - 1) + tile, F32),
        pltpu.VMEM((norms,) + tile, F32),
        pltpu.VMEM(tile, F32),
        pltpu.VMEM(tile, jnp.int32),
        pltpu.VMEM(tile, jnp.int32),
        pltpu.SMEM(tile, jnp.int32),
        pltpu.VMEM(davidson_mix.shape, F32),
        pltpu.SemaphoreType.DMA((3,)),
        pltpu.SemaphoreType.DMA((2, count)),
        pltpu.SemaphoreType.DMA((2, count, 2, 20)),
        pltpu.SemaphoreType.DMA((norms, 2, RING - 1)),
        pltpu.SemaphoreType.DMA((norms, 2, RING - 1)),
        pltpu.SemaphoreType.DMA((3 + count,)),
        pltpu.SemaphoreType.DMA((3 + count,)),
        pltpu.SemaphoreType.DMA,
        pltpu.SemaphoreType.DMA((count,)),
        pltpu.SemaphoreType.REGULAR,
    ]
    flops = (PRODUCTS + 1) * 2 * terms * 2 * width**3
    updated, handed = pl.pallas_call(
        kernel,
        out_shape=(
            jax.ShapeDtypeStruct(wavefunction.shape, BF16),
            jax.ShapeDtypeStruct(left_env.shape, BF16),
        ),
        in_specs=[vmem, anywhere, anywhere, smem, smem, anywhere, smem],
        out_specs=(vmem, anywhere),
        scratch_shapes=scratch,
        compiler_params=pltpu.CompilerParams(
            collective_id=0, has_side_effects=True, vmem_limit_bytes=60 * 2**20
        ),
        cost_estimate=pl.CostEstimate(flops=flops, bytes_accessed=40 * 2**20, transcendentals=0),
        name="davidson_update",
    )(wavefunction, left_env, right_env, source, block_sizes, davidson_mix, ritz_weights)
    return keep(updated, handed)


def solution(mesh):
    in_specs = (
        P("chain", "bond", None, None),
        P("chain", "bond", None, None, None),
        P("chain", "bond", None, None, None),
        P("chain", "bond", None),
        P("chain", "bond"),
        P("chain", None, None),
        P("chain", None),
    )
    out_specs = (P("chain", "bond", None, None), P("chain", "bond", None, None, None))
    return jax.shard_map(body, mesh=mesh, in_specs=in_specs, out_specs=out_specs, check_vma=False)
```
